32 devices in a mesh: group: 2 (over core), dp: 4 (over y, x), tensor: 4 (over z).
Axes of the slice: x: 2, y: 2, z: 4, core: 2. Of those that a mesh axis runs over, the one named last changes fastest.
Arguments:
- stream: bfloat16 [32, 8192], P('tensor', ('group', 'dp'))
- norm_attn: bfloat16 [8192], P(('group', 'dp')), may hold values from 0.29882812 to 3
- norm_ffn: bfloat16 [8192], P(('group', 'dp')), may hold values from 0.29882812 to 3
- w_query: bfloat16 [8192, 8192], P(('group', 'dp'), 'tensor'), may hold values from -0.0625 to 0.0625
- w_keyval: bfloat16 [8192, 2048], P(('group', 'dp'), 'tensor'), may hold values from -0.0625 to 0.0625
- w_out: bfloat16 [8192, 8192], P('tensor', ('group', 'dp')), may hold values from -0.0625 to 0.0625
- w_gate: bfloat16 [8192, 28672], P(('group', 'dp'), 'tensor'), may hold values from -0.0625 to 0.0625
- w_up: bfloat16 [8192, 28672], P(('group', 'dp'), 'tensor'), may hold values from -0.0625 to 0.0625
- w_down: bfloat16 [28672, 8192], P('tensor', ('group', 'dp')), may hold values from -0.03125 to 0.03125
- cache: bfloat16 [32, 8, 256, 256], P(('group', 'dp'), 'tensor')
- lengths: int32 [32], P(('group', 'dp')), may hold values from 1 to 256, as said below
- location: int32 [32], P(('group', 'dp')), may hold values from 0 to 31, as said below
Outputs:
- updated: float32 [32, 8192], P('tensor', ('group', 'dp'))
The draws below stay inside these ranges and needn't reach their ends.
Inputs may be any that keep to these rules, and one draw needn't show every extreme that they name: Each of the 32 slots is named by exactly one request. Slot s belongs to owner s // 4. Requests r of one aligned block of 4 (one device's requests) that share an owner have different values of location modulo 2; in every draw 2 of them share an owner. `lengths`: some slot holds 256 valid positions in every draw.
All inputs are finite; a program needn't handle non-finite values.
Results may differ from the reference program's by a relative error of at most 0.005.
The reference program's roundings to bfloat16 on the way count: a program that leaves them out, or rounds other values in their place, can miss the bound.
Values may be sent and summed in bfloat16 or wider, within the bound.
A program may use at most 128 MiB of HBM per device.

```python
import math
import jax
import jax.numpy as jnp
from jax import lax

D = 8192
H = 64
KVH = 8
HD = 128
FF = 28672
CTX = 256
CAP = 2
OWNERS = 8
REQ_DEV = 4
REQUESTS = 32


def draw_stream(key, part):
    first = jax.random.fold_in(key, 0)
    column = jnp.arange(D, dtype=jnp.float32)
    lift = jnp.exp(jnp.log(3.0) * column / D) / 1.7
    base = jax.random.normal(first, (REQUESTS, D), jnp.float32)
    return (base * lift[None, :]).astype(jnp.bfloat16)


def draw_cache(key, part):
    first = jax.random.fold_in(key, 0)
    shape = (REQUESTS, KVH, CTX, 2 * HD)
    base = jax.random.normal(first, shape, jnp.float32)
    return base.astype(jnp.bfloat16)


def draw_lengths(key, part):
    first, second = jax.random.split(key)
    values = jax.random.randint(first, (REQUESTS,), 1, CTX + 1)
    chosen = jax.random.randint(second, (), 0, REQUESTS)
    return values.at[chosen].set(CTX).astype(jnp.int32)


def draw_location(key, part):
    first, second = jax.random.split(key)
    groups = REQ_DEV // CAP
    shuffled = jax.random.permutation(first, OWNERS).astype(jnp.int32)
    forced = (shuffled == 1) | (shuffled == OWNERS - 1) | (shuffled == OWNERS // 2)
    priority = jnp.where(forced, -1, jnp.arange(OWNERS, dtype=jnp.int32))
    picked_order = jnp.argsort(priority, stable=True)
    offsets = shuffled[picked_order][:groups]
    device_keys = jax.random.split(second, OWNERS)
    order = jax.vmap(lambda single: jax.random.permutation(single, REQ_DEV))(device_keys)
    source = jnp.arange(OWNERS, dtype=jnp.int32)[:, None]
    group_index = order // CAP
    within = order % CAP
    owner = (source + offsets[group_index]) % OWNERS
    return (owner * REQ_DEV + group_index * CAP + within).reshape(-1).astype(jnp.int32)


def block_scale(stream_key, extent, shards, least, high):
    factor_of, own = 1.0, jax.random.fold_in(stream_key, 6)
    for position, parts in shards:
        heights = jnp.exp(jax.random.uniform(jax.random.fold_in(own, position), (parts,), jnp.float32, least / len(shards), high / len(shards)))
        factor_of = factor_of * jnp.repeat(heights, extent[position] // parts).reshape([-1 if axis == position else 1 for axis in range(len(extent))])
    return factor_of


def normal_values(rng, shape, scale, reach, cuts=(), held_as=jnp.bfloat16):
    loudness = block_scale(rng, shape, cuts, -0.22, 0.18) if cuts else 1.0
    result = jax.random.normal(rng, shape, jnp.float32) * scale * loudness
    return jnp.minimum(jnp.maximum(result, -reach), reach).astype(held_as)


def setup_inputs(seed: int = 0) -> dict:
    key_of = jax.random.split(jax.random.key(seed), 13)
    stream = draw_stream(jax.random.fold_in(key_of[12], 71), 0)
    norm_attn = jnp.clip(jnp.exp(math.log(3.0) - 2.306499 * jax.random.uniform(key_of[1], (D,), jnp.float32) ** block_scale(key_of[1], (D,), ((0, 8),), -0.2, 0.2)), 0.29882812, 3.0).astype(jnp.bfloat16)
    norm_ffn = jnp.clip(jnp.exp(math.log(3.0) - 2.306499 * jax.random.uniform(key_of[2], (D,), jnp.float32) ** block_scale(key_of[2], (D,), ((0, 8),), -0.2, 0.2)), 0.29882812, 3.0).astype(jnp.bfloat16)
    w_query = normal_values(key_of[3], (D, H * HD), D ** -0.5, 0.0625, ((0, 8), (1, 4)))
    w_keyval = normal_values(key_of[4], (D, 2 * KVH * HD), D ** -0.5, 0.0625, ((0, 8), (1, 4)))
    w_out = normal_values(key_of[5], (H * HD, D), (H * HD) ** -0.5, 0.0625, ((0, 4), (1, 8)))
    w_gate = normal_values(key_of[6], (D, FF), D ** -0.5, 0.0625, ((0, 8), (1, 4)))
    w_up = normal_values(key_of[7], (D, FF), D ** -0.5, 0.0625, ((0, 8), (1, 4)))
    w_down = normal_values(key_of[8], (FF, D), FF ** -0.5, 0.03125, ((0, 4), (1, 8)))
    cache = draw_cache(jax.random.fold_in(key_of[12], 71), 0)
    lengths = draw_lengths(jax.random.fold_in(key_of[12], 71), 0)
    location = draw_location(jax.random.fold_in(key_of[12], 71), 0)
    return {"stream": stream, "norm_attn": norm_attn, "norm_ffn": norm_ffn, "w_query": w_query, "w_keyval": w_keyval, "w_out": w_out, "w_gate": w_gate, "w_up": w_up, "w_down": w_down, "cache": cache, "lengths": lengths, "location": location}


EPSILON = 1e-05

def normed(values, gain):
    squares = lax.optimization_barrier(jnp.sum(values * values, axis=1, keepdims=True))
    return (values * lax.rsqrt(squares / D + EPSILON) * gain.astype(jnp.float32)[None, :]).astype(jnp.bfloat16)

def attend(query, fresh, stored, counts):
    items = query.shape[0]
    grouped = query.reshape(items, KVH, H // KVH, HD).astype(jnp.float32)
    fresh = fresh.reshape(items, KVH, 2 * HD).astype(jnp.float32)
    stored = stored.astype(jnp.float32)
    scale = HD ** (-0.5)
    scores = jnp.einsum('mkgd,mkpd->mkgp', grouped, stored[..., :HD]) * scale
    own = jnp.einsum('mkgd,mkd->mkg', grouped, fresh[..., :HD]) * scale
    place = jnp.arange(CTX, dtype=jnp.int32)
    valid = place[None, None, None, :] < counts[:, None, None, None]
    top = jnp.maximum(lax.optimization_barrier(jnp.max(jnp.where(valid, scores, -1e+30), axis=3)), own)
    expo = jnp.where(valid, jnp.exp(scores - top[..., None]), 0.0)
    own_expo = jnp.exp(own - top)
    total = lax.optimization_barrier(jnp.sum(expo, axis=3)) + own_expo
    probs = lax.optimization_barrier((expo / total[..., None]).astype(jnp.bfloat16)).astype(jnp.float32)
    own_prob = lax.optimization_barrier((own_expo / total).astype(jnp.bfloat16)).astype(jnp.float32)
    mixed = jnp.einsum('mkgp,mkpd->mkgd', probs, stored[..., HD:])
    mixed = mixed + own_prob[..., None] * fresh[:, :, None, HD:]
    return mixed.reshape(items, H * HD).astype(jnp.bfloat16)

def reference(stream, norm_attn, norm_ffn, w_query, w_keyval, w_out, w_gate, w_up, w_down, cache, lengths, location):
    resid = stream.astype(jnp.float32)
    attn_in = normed(resid, norm_attn)
    query = jnp.dot(attn_in, w_query, preferred_element_type=jnp.float32).astype(jnp.bfloat16)
    fresh = jnp.dot(attn_in, w_keyval, preferred_element_type=jnp.float32).astype(jnp.bfloat16)

    def one_block(pieces):
        block_query, block_fresh, block_slot = pieces
        return attend(block_query, block_fresh, cache[block_slot], lengths[block_slot])
    attended = lax.map(one_block, (query.reshape(OWNERS, REQ_DEV, H * HD), fresh.reshape(OWNERS, REQ_DEV, 2 * KVH * HD), location.reshape(OWNERS, REQ_DEV)))
    attended = attended.reshape(REQUESTS, H * HD)
    middle = resid + jnp.dot(attended, w_out, preferred_element_type=jnp.float32)
    ffn_in = normed(middle, norm_ffn)
    gate = jnp.dot(ffn_in, w_gate, preferred_element_type=jnp.float32)
    upper = jnp.dot(ffn_in, w_up, preferred_element_type=jnp.float32)
    hidden = (jax.nn.silu(gate) * upper).astype(jnp.bfloat16)
    return middle + jnp.dot(hidden, w_down, preferred_element_type=jnp.float32)
```

```python
import jax
import jax.numpy as jnp
from jax import lax
from jax.sharding import PartitionSpec as P

D = 8192


EPSILON = 1e-05


def normed(values, gain):
    squares = lax.psum(jnp.sum(values * values, axis=1), ("group", "dp"))
    scale = lax.rsqrt(squares / D + EPSILON)
    return (values * scale[:, None] * gain.astype(jnp.float32)[None, :]).astype(jnp.bfloat16)


def width_sum(normal_rows, matrices, order=None):
    gathered = lax.all_gather(normal_rows, "tensor", axis=0, tiled=True)
    if order is not None:
        gathered = permuted(order, gathered)
    return lax.psum_scatter(
        jnp.concatenate(
            [jnp.dot(gathered, matrix, preferred_element_type=jnp.float32) for matrix in matrices],
            axis=1,
        ),
        ("group", "dp"),
        scatter_dimension=0,
        tiled=True,
    )


def project_rows(local_rows, matrix, order=None):
    gathered = lax.all_gather(local_rows, ("group", "dp"), axis=0, tiled=True)
    if order is not None:
        gathered = permuted(order, gathered)
    partial_sum = jnp.dot(gathered, matrix, preferred_element_type=jnp.float32)
    return lax.psum_scatter(partial_sum, "tensor", scatter_dimension=0, tiled=True)


def permuted(order, rows):
    return jnp.dot(order, rows, preferred_element_type=jnp.float32).astype(rows.dtype)


def attend(query, fresh, stored, counts):
    items = query.shape[0]
    kv_local = stored.shape[1]
    head_size = stored.shape[3] // 2
    grouped = query.reshape(items, kv_local, -1, head_size)
    fresh = fresh.reshape(items, kv_local, 2 * head_size)
    scale = head_size ** (-0.5)
    scores = (
        jnp.einsum(
            "mkgd,mkpd->mkgp", grouped, stored[..., :head_size], preferred_element_type=jnp.float32
        )
        * scale
    )
    own = (
        jnp.einsum(
            "mkgd,mkd->mkg", grouped, fresh[..., :head_size], preferred_element_type=jnp.float32
        )
        * scale
    )
    place = jnp.arange(stored.shape[2], dtype=jnp.int32)
    valid = place[None, None, None, :] < counts[:, None, None, None]
    top = jnp.maximum(jnp.max(jnp.where(valid, scores, -1e30), axis=3), own)
    expo = jnp.where(valid, jnp.exp(scores - top[..., None]), 0.0)
    own_expo = jnp.exp(own - top)
    total = jnp.sum(expo, axis=3) + own_expo
    probs = (expo / total[..., None]).astype(jnp.bfloat16)
    own_prob = (own_expo / total).astype(jnp.bfloat16)
    mixed = jnp.einsum(
        "mkgp,mkpd->mkgd", probs, stored[..., head_size:], preferred_element_type=jnp.float32
    )
    mixed = mixed + own_prob.astype(jnp.float32)[..., None] * fresh[:, :, None, head_size:].astype(
        jnp.float32
    )
    return mixed.reshape(items, -1).astype(jnp.bfloat16)


def per_device(
    stream,
    norm_attn,
    norm_ffn,
    w_query,
    w_keyval,
    w_out,
    w_gate,
    w_up,
    w_down,
    cache,
    lengths,
    location,
):
    resid = stream.astype(jnp.float32)
    attn_in = normed(resid, norm_attn)
    places = lax.all_gather(location, ("group", "dp"), axis=0, tiled=True)
    slots = jnp.arange(places.shape[0], dtype=jnp.int32)
    by_slot = (slots[:, None] == places[None, :]).astype(jnp.bfloat16)
    by_request = (places[:, None] == slots[None, :]).astype(jnp.bfloat16)
    joined = width_sum(attn_in, (w_query, w_keyval), by_slot)
    query_cols = w_query.shape[1]
    query = joined[:, :query_cols].astype(jnp.bfloat16)
    fresh = joined[:, query_cols:].astype(jnp.bfloat16)
    attended = attend(query, fresh, cache, lengths)
    middle = resid + project_rows(attended, w_out, by_request)
    ffn_in = normed(middle, norm_ffn)
    both = width_sum(ffn_in, (w_gate, w_up))
    hidden_cols = w_gate.shape[1]
    hidden = (jax.nn.silu(both[:, :hidden_cols]) * both[:, hidden_cols:]).astype(jnp.bfloat16)
    return middle + project_rows(hidden, w_down)


def solution(mesh):
    placed = (
        P("tensor", ("group", "dp")),
        P(("group", "dp")),
        P(("group", "dp")),
        P(("group", "dp"), "tensor"),
        P(("group", "dp"), "tensor"),
        P("tensor", ("group", "dp")),
        P(("group", "dp"), "tensor"),
        P(("group", "dp"), "tensor"),
        P("tensor", ("group", "dp")),
        P(("group", "dp"), "tensor", None, None),
        P(("group", "dp")),
        P(("group", "dp")),
    )
    return jax.shard_map(
        per_device,
        mesh=mesh,
        in_specs=placed,
        out_specs=P("tensor", ("group", "dp")),
        check_vma=False,
    )
```
